32 devices in a mesh: layer: 8 (over z, x), tok: 4 (over y, core).
Axes of the slice: x: 2, y: 2, z: 4, core: 2. Of those that a mesh axis runs over, the one named last changes fastest.
Arguments:
- acts: bfloat16 [8, 128, 2048], P('layer', 'tok'), may hold values from -6 to 6
- w_enc: bfloat16 [8, 2048, 1024], P('layer', 'tok'), may hold values from -0.125 to 0.125
- b_enc: float32 [8, 1024], P('layer'), may hold values from -0.5 to 0.5
- w_dec: bfloat16 [8, 8, 1024, 2048], P('layer', None, None, 'tok'), may hold values from -0.0625 to 0.0625
- targets: bfloat16 [8, 128, 2048], P('layer', None, 'tok'), may hold values from -6 to 6
Outputs:
- code_grad: float32 [8, 128, 1024], P('layer', 'tok')
- dec_grad: bfloat16 [8, 8, 1024, 2048], P('layer', None, None, 'tok')
The draws below stay inside these ranges and needn't reach their ends.
All inputs are finite; a program needn't handle non-finite values.
Results may differ from the reference program's by a relative error of at most 0.0034.
Values may be sent and summed in bfloat16 or wider, within the bound.
A program may use at most 64 MiB of HBM per device.

```python
import jax
import jax.numpy as jnp
from jax import lax

D = 2048
F = 1024
TOKENS = 128
LAYERS = 8


def block_levels(key, shape, shards, low, top_value):
    level = 1.0
    for position, parts in shards:
        steps = jax.random.uniform(jax.random.fold_in(jax.random.fold_in(key, 6), position), (parts,), jnp.float32, low / len(shards), top_value / len(shards))
        level = level * jnp.repeat(jnp.exp(steps), shape[position] // parts).reshape((-1,) + (1,) * (len(shape) - 1 - position))
    return level


def bell_draw(own_key, shape, width, limit, shards=(), dtype=jnp.bfloat16):
    gain = block_levels(own_key, shape, shards, -0.22, 0.18) if shards else 1.0
    result = jax.random.normal(own_key, shape, jnp.float32) * width * gain
    return jnp.minimum(jnp.maximum(result, -limit), limit).astype(dtype)


def setup_inputs(seed: int = 0) -> dict:
    streams_of = jax.random.split(jax.random.key(seed), 6)
    return {
        "acts": bell_draw(streams_of[0], (LAYERS, TOKENS, D), 1.0, 6.0, ((0, 8), (1, 4))),
        "w_enc": bell_draw(streams_of[1], (LAYERS, D, F), D ** -0.5, 0.125, ((0, 8), (1, 4))),
        "b_enc": jnp.clip(jax.random.uniform(streams_of[2], (LAYERS, F), jnp.float32, -0.5, 0.5) * block_levels(streams_of[2], (LAYERS, F), ((0, 8),), -0.4, 0.0), -0.5, 0.5),
        "w_dec": bell_draw(streams_of[3], (LAYERS, LAYERS, F, D), (F * LAYERS) ** -0.5, 0.0625, ((0, 8), (3, 4))),
        "targets": bell_draw(streams_of[4], (LAYERS, TOKENS, D), 1.0, 6.0, ((0, 8), (2, 4))),
    }


def reference(acts, w_enc, b_enc, w_dec, targets):
    layers = w_dec.shape[0]
    layer_order = jnp.arange(layers)
    pair_live = layer_order[:, None] <= layer_order[None, :]

    def encode(inputs):
        source, weight, bias = inputs
        preact = jnp.dot(source, weight, preferred_element_type=jnp.float32) + bias
        return jnp.maximum(preact, 0.0).astype(jnp.bfloat16)

    feature_codes = lax.map(encode, (acts, w_enc, b_enc))

    def forward(total, inputs):
        source, dec_slabs, pair_keep = inputs
        masked = jnp.where(pair_keep[:, None, None], dec_slabs.astype(jnp.float32), 0.0)
        product = jnp.einsum("tf,jfd->jtd", source.astype(jnp.float32), masked, precision=lax.Precision.HIGHEST)
        return total + product, None

    empty_sum = jnp.zeros((layers, TOKENS, D), jnp.float32)
    rebuilt, _ = lax.scan(forward, empty_sum, (feature_codes, w_dec, pair_live))
    errors_wide = rebuilt - targets.astype(jnp.float32)

    def backward(inputs):
        source, dec_slabs, pair_keep = inputs
        masked = jnp.where(pair_keep[:, None, None], dec_slabs.astype(jnp.float32), 0.0)
        weight_grad = jnp.einsum("tf,jtd->jfd", source.astype(jnp.float32), errors_wide, precision=lax.Precision.HIGHEST)
        weight_grad = jnp.where(pair_keep[:, None, None], weight_grad, 0.0).astype(jnp.bfloat16)
        code_part = jnp.einsum("jtd,jfd->tf", errors_wide, masked, precision=lax.Precision.HIGHEST)
        return code_part, weight_grad

    code_grad, dec_grad = lax.map(backward, (feature_codes, w_dec, pair_live))
    return code_grad, dec_grad
```

```python
import functools

import jax
import jax.numpy as jnp
from jax import lax
from jax.experimental import pallas as pl
from jax.experimental.pallas import tpu as pltpu
from jax.sharding import PartitionSpec as P

MESH = pl.DeviceIdType.MESH
BF = jnp.bfloat16
F32 = jnp.float32


def exchange(
    n, t, acts, w_enc, bias, w_dec, targets,
    codes, errs, grads,
    acts_v, wenc_v, wdec_v, pre, pre_in, pair_out, pair_in, codes_v,
    held, mix_out, mix_in, fwd_out, fwd_in, bwd_out, bwd_in, err_v,
    cg, cg_in, cg_out, cg_far,
    s_wenc, s_wdec, s_acts, a_send, a_recv, p_sem, y_send, y_recv, c_sem,
    m_send, m_recv, f_send, f_recv, b_send, b_recv, e_send, e_recv, g_sem, gy_send, gy_recv,
):
    groups, chips = n // 2, t // 2
    i, k = lax.axis_index("layer"), lax.axis_index("tok")
    g, p = i // 2, i % 2
    y, c = k // 2, k % 2
    other_layer = 2 * g + 1 - p
    other_core = 2 * y + 1 - c
    rows, depth = acts.shape[1], wenc_v.shape[0]
    features, width = wdec_v.shape[1], wdec_v.shape[2]
    half_f, half_w = features // 2, width // 2
    tokens = rows * t
    first = 2 * g
    count = n - first

    def remote(src, dst, send, recv, layer, tok):
        return pltpu.make_async_remote_copy(
            src_ref=src, dst_ref=dst, send_sem=send, recv_sem=recv,
            device_id=(layer, tok), device_id_type=MESH,
        )

    wenc_copy = pltpu.make_async_copy(w_enc.at[0], wenc_v, s_wenc)
    wenc_copy.start()
    own_cols = pl.ds(pl.multiple_of(k * depth, depth), depth)
    own_rows = pl.ds(pl.multiple_of(k * rows, rows), rows)
    acts_copy = pltpu.make_async_copy(acts.at[0, :, own_cols], acts_v.at[own_rows, :], s_acts)
    acts_copy.start()

    def dec_copy(j):
        return pltpu.make_async_copy(w_dec.at[0, j], wdec_v.at[j], s_wdec.at[j])

    barrier = pltpu.get_barrier_semaphore()
    for step in range(1, t):
        pl.semaphore_signal(
            barrier, inc=1, device_id=(i, lax.rem(k + step, t)), device_id_type=MESH
        )
    pl.semaphore_signal(barrier, inc=1, device_id=(other_layer, k), device_id_type=MESH)

    @pl.when(g > 0)
    def _():
        pl.semaphore_signal(barrier, inc=1, device_id=(i - 2, k), device_id_type=MESH)

    @pl.when(g < groups - 1)
    def _():
        pl.semaphore_signal(barrier, inc=1, device_id=(i + 2, k), device_id_type=MESH)

    @pl.when(g == 0)
    def _():
        fwd_in[...] = jnp.zeros_like(fwd_in)

    for q in range(2):
        bwd_in[first + q] = jnp.zeros(bwd_in.shape[1:], BF)

    linked = (g > 0).astype(jnp.int32) + (g < groups - 1).astype(jnp.int32)
    pl.semaphore_wait(barrier, t + linked)

    def acts_send(peer):
        cols = pl.ds(pl.multiple_of(peer * depth, depth), depth)
        return remote(
            acts.at[0, :, cols], acts_v.at[own_rows, :], a_send.at[peer], a_recv.at[k], i, peer
        )

    def acts_land(peer):
        lines = pl.ds(pl.multiple_of(peer * rows, rows), rows)
        return remote(
            acts.at[0, :, own_cols], acts_v.at[lines, :], a_send.at[peer], a_recv.at[peer], i, peer
        )

    for step in range(1, t):
        acts_send(lax.rem(k + step, t)).start()

    def start_dec(q, _):
        dec_copy(n - 1 - q).start()
        return 0

    lax.fori_loop(0, count, start_dec, 0)
    wenc_copy.wait()
    acts_copy.wait()
    for step in range(1, t):
        acts_land(lax.rem(k + step, t)).wait_recv()

    for h in range(2):
        pre[h] = jnp.dot(
            acts_v[...], wenc_v[:, h * half_f:(h + 1) * half_f], preferred_element_type=F32
        )
    pre_copy = remote(pre.at[1 - c], pre_in, p_sem.at[0], p_sem.at[1], i, other_core)
    pre_copy.start()
    pre_copy.wait_recv()
    chip_sum = pre[c] + pre_in[...]
    pair_out[...] = chip_sum.astype(BF)

    def pair_send(peer):
        return remote(pair_out, pair_in.at[y], y_send.at[peer], y_recv.at[y], i, 2 * peer + c)

    def pair_land(peer):
        return remote(pair_out, pair_in.at[peer], y_send.at[peer], y_recv.at[peer], i, 2 * peer + c)

    for step in range(1, chips):
        pair_send(lax.rem(y + step, chips)).start()
    pre_in[...] = chip_sum + bias[pl.ds(c, 1), :]
    for step in range(1, chips):
        peer = lax.rem(y + step, chips)
        pair_land(peer).wait_recv()
        pre_in[...] += pair_in[peer].astype(F32)
    codes_v[c] = jnp.maximum(pre_in[...], 0.0).astype(BF)
    codes_copy = remote(codes_v.at[c], codes_v.at[c], c_sem.at[0], c_sem.at[1], i, other_core)
    codes_copy.start()
    codes_land = remote(
        codes_v.at[c], codes_v.at[1 - c], c_sem.at[0], c_sem.at[1], i, other_core
    )
    codes_land.wait_recv()
    codes[...] = codes_v[...]

    def mix(j):
        return remote(mix_out.at[j], mix_in.at[j], m_send.at[j], m_recv.at[j], other_layer, k)

    def ahead(j):
        return remote(fwd_out.at[j], fwd_in.at[j], f_send.at[j], f_recv.at[j], i + 2, k)

    def back(j):
        return remote(bwd_out.at[j], bwd_in.at[j], b_send.at[j], b_recv.at[j], i - 2, k)

    def share(j):
        return remote(err_v.at[j, p], err_v.at[j, p], e_send.at[j], e_recv.at[j], other_layer, k)

    def share_land(j):
        return remote(
            err_v.at[j, p], err_v.at[j, 1 - p], e_send.at[j], e_recv.at[j], other_layer, k
        )

    def decode(q, _):
        j = n - 1 - q
        dec_copy(j).wait()
        both = []
        for h in range(2):
            cols = slice(h * half_w, (h + 1) * half_w)
            product = jnp.dot(
                codes_v[0], wdec_v[j, :half_f, cols], preferred_element_type=F32
            ) + jnp.dot(codes_v[1], wdec_v[j, half_f:, cols], preferred_element_type=F32)
            product = jnp.where(j >= i, product, 0.0)
            goal = targets[0, :, cols].astype(F32)
            both.append(product - jnp.where(j == i, goal, 0.0))
        held[j] = jnp.where(p == 0, both[0], both[1])
        mix_out[j] = jnp.where(p == 0, both[1], both[0]).astype(BF)
        mix(j).start()
        return 0

    lax.fori_loop(0, count, decode, 0)

    def gather_pair(j):
        mix(j).wait_recv()
        held[j] = held[j] + mix_in[j].astype(F32)

    def wait_ahead(j):
        @pl.when(g > 0)
        def _():
            ahead(j).wait_recv()

    def wait_back(j):
        @pl.when(j >= first + 2)
        def _():
            back(j).wait_recv()

    def send_ahead(j):
        @pl.when(j >= first + 2)
        def _():
            fwd_out[j] = (held[j] + fwd_in[j].astype(F32)).astype(BF)
            ahead(j).start()

    def send_back(j):
        @pl.when(g > 0)
        def _():
            bwd_out[j] = (held[j] + bwd_in[j].astype(F32)).astype(BF)
            back(j).start()

    def finish(j):
        total = held[j] + fwd_in[j].astype(F32) + bwd_in[j].astype(F32)
        err_v[j, p] = total.astype(BF)
        share(j).start()

    @pl.when(g < groups // 2)
    def _():
        def one(q, _):
            j = n - 1 - q
            gather_pair(j)
            wait_ahead(j)
            send_ahead(j)
            return 0

        def two(q, _):
            j = n - 1 - q
            wait_back(j)
            send_back(j)
            finish(j)
            return 0

        lax.fori_loop(0, count, one, 0)
        lax.fori_loop(0, count, two, 0)

    @pl.when(g >= groups // 2)
    def _():
        def one(q, _):
            j = n - 1 - q
            gather_pair(j)
            wait_back(j)
            send_back(j)
            return 0

        def two(q, _):
            j = n - 1 - q
            wait_ahead(j)
            send_ahead(j)
            finish(j)
            return 0

        lax.fori_loop(0, count, one, 0)
        lax.fori_loop(0, count, two, 0)

    cg[...] = jnp.zeros_like(cg)

    def backward(q, _):
        j = n - 1 - q
        share_land(j).wait_recv()
        keep = j >= i
        errs[j] = jnp.where(keep, err_v[j], jnp.zeros_like(err_v[j]))

        @pl.when(keep)
        def _():
            nt = (((1,), (1,)), ((), ()))
            part = lax.dot_general(
                err_v[j, 0], wdec_v[j, :, :half_w], nt, preferred_element_type=F32
            ) + lax.dot_general(
                err_v[j, 1], wdec_v[j, :, half_w:], nt, preferred_element_type=F32
            )
            cg[...] += part.reshape(cg.shape)

        return 0

    lax.fori_loop(0, count, backward, 0)

    def blank(j, _):
        errs[j] = jnp.zeros(errs.shape[1:], BF)
        return 0

    lax.fori_loop(0, first, blank, 0)

    cg_copy = remote(cg.at[:, 1 - c], cg_in, g_sem.at[0], g_sem.at[1], i, other_core)
    cg_copy.start()
    cg_copy.wait_recv()

    def far_send(peer):
        return remote(
            cg_out.at[peer], cg_far.at[y], gy_send.at[peer], gy_recv.at[y], i, 2 * peer + c
        )

    def far_land(peer):
        return remote(
            cg_out.at[peer], cg_far.at[peer], gy_send.at[peer], gy_recv.at[peer], i, 2 * peer + c
        )

    for step in range(1, chips):
        peer = lax.rem(y + step, chips)
        cg_out[peer] = (cg[peer, c] + cg_in[peer]).astype(BF)
        far_send(peer).start()
    grads[...] = cg[y, c] + cg_in[y]
    for step in range(1, chips):
        peer = lax.rem(y + step, chips)
        far_land(peer).wait_recv()
        grads[...] += cg_far[peer].astype(F32)

    for step in range(1, t):
        acts_send(lax.rem(k + step, t)).wait_send()
    pre_copy.wait_send()
    codes_copy.wait_send()
    cg_copy.wait_send()
    for step in range(1, chips):
        peer = lax.rem(y + step, chips)
        pair_send(peer).wait_send()
        far_send(peer).wait_send()

    def drain(q, _):
        j = n - 1 - q
        mix(j).wait_send()
        share(j).wait_send()

        @pl.when(j >= first + 2)
        def _():
            ahead(j).wait_send()

        @pl.when(g > 0)
        def _():
            back(j).wait_send()

        return 0

    lax.fori_loop(0, count, drain, 0)


def weight_grads(codes, errs, grads_in, dec, grads):
    grads[...] = grads_in[...]
    tn = (((0,), (0,)), ((), ()))
    half_f, half_w = codes.shape[2], errs.shape[3]
    for a in range(2):
        for b in range(2):
            dec[0, 0, a * half_f:(a + 1) * half_f, b * half_w:(b + 1) * half_w] = lax.dot_general(
                codes[a], errs[0, b], tn, preferred_element_type=F32
            ).astype(BF)


def local(acts, w_enc, b_enc, w_dec, targets):
    n, t = lax.axis_size("layer"), lax.axis_size("tok")
    _, rows, model = acts.shape
    _, depth, features = w_enc.shape
    width = w_dec.shape[3]
    tokens = rows * t
    half_f, half_w = features // 2, width // 2
    chips = t // 2
    vmem = pl.BlockSpec(memory_space=pltpu.VMEM)
    hbm = pl.BlockSpec(memory_space=pl.ANY)
    block = (n, tokens, half_w)
    dma = pltpu.SemaphoreType.DMA
    codes, errs, grads = pl.pallas_call(
        functools.partial(exchange, n, t),
        out_shape=(
            jax.ShapeDtypeStruct((2, tokens, half_f), BF),
            jax.ShapeDtypeStruct((n, 2, tokens, half_w), BF),
            jax.ShapeDtypeStruct((rows, features), F32),
        ),
        in_specs=[hbm, hbm, vmem, hbm, vmem],
        out_specs=(vmem, vmem, vmem),
        scratch_shapes=[
            pltpu.VMEM((tokens, depth), BF),
            pltpu.VMEM((depth, features), BF),
            pltpu.VMEM((n, features, width), BF),
            pltpu.VMEM((2, tokens, half_f), F32),
            pltpu.VMEM((tokens, half_f), F32),
            pltpu.VMEM((tokens, half_f), BF),
            pltpu.VMEM((chips, tokens, half_f), BF),
            pltpu.VMEM((2, tokens, half_f), BF),
            pltpu.VMEM(block, F32),
            pltpu.VMEM(block, BF),
            pltpu.VMEM(block, BF),
            pltpu.VMEM(block, BF),
            pltpu.VMEM(block, BF),
            pltpu.VMEM(block, BF),
            pltpu.VMEM(block, BF),
            pltpu.VMEM((n, 2, tokens, half_w), BF),
            pltpu.VMEM((chips, 2, rows, features), F32),
            pltpu.VMEM((chips, rows, features), F32),
            pltpu.VMEM((chips, rows, features), BF),
            pltpu.VMEM((chips, rows, features), BF),
            dma, dma((n,)), dma, dma((t,)), dma((t,)), dma((2,)),
            dma((chips,)), dma((chips,)), dma((2,)),
            dma((n,)), dma((n,)), dma((n,)), dma((n,)), dma((n,)), dma((n,)),
            dma((n,)), dma((n,)), dma((2,)), dma((chips,)), dma((chips,)),
        ],
        compiler_params=pltpu.CompilerParams(
            collective_id=0, has_side_effects=True, vmem_limit_bytes=56 * 2**20
        ),
        name="exchange",
    )(acts, w_enc, b_enc.reshape(2, half_f), w_dec, targets)
    dec, code_share = pl.pallas_call(
        weight_grads,
        grid=(n,),
        out_shape=(
            jax.ShapeDtypeStruct((1, n, features, width), BF),
            jax.ShapeDtypeStruct((rows, features), F32),
        ),
        in_specs=[
            pl.BlockSpec((2, tokens, half_f), lambda j: (0, 0, 0)),
            pl.BlockSpec((1, 2, tokens, half_w), lambda j: (j, 0, 0, 0)),
            pl.BlockSpec((rows, features), lambda j: (0, 0)),
        ],
        out_specs=(
            pl.BlockSpec((1, 1, features, width), lambda j: (0, j, 0, 0)),
            pl.BlockSpec((rows, features), lambda j: (0, 0)),
        ),
        compiler_params=pltpu.CompilerParams(vmem_limit_bytes=40 * 2**20),
        name="weight_grads",
    )(codes, errs, grads)
    return (code_share[None], dec)


def solution(mesh):
    return jax.shard_map(
        local,
        mesh=mesh,
        in_specs=(
            P("layer", "tok", None),
            P("layer", "tok", None),
            P("layer", None),
            P("layer", None, None, "tok"),
            P("layer", None, "tok"),
        ),
        out_specs=(P("layer", "tok", None), P("layer", None, None, "tok")),
        check_vma=False,
    )
```

```python
import functools

import jax
import jax.numpy as jnp
from jax import lax
from jax.experimental import pallas as pl
from jax.experimental.pallas import tpu as pltpu
from jax.sharding import PartitionSpec as P

MESH = pl.DeviceIdType.MESH
BF = jnp.bfloat16
F32 = jnp.float32


def exchange(
    n, t, acts, w_enc, bias, w_dec, targets,
    codes, errs, grads,
    acts_v, wenc_v, wdec_v, pre, pre_in, pair_out, pair_in, codes_v,
    held, mix_out, mix_in, fwd_out, fwd_in, bwd_out, bwd_in, err_v,
    cg, cg_in, cg_out, cg_far,
    s_wenc, s_wdec, s_acts, a_send, a_recv, p_sem, y_send, y_recv, c_sem,
    m_send, m_recv, f_send, f_recv, b_send, b_recv, e_send, e_recv, d_send, d_recv, g_sem, gy_send, gy_recv,
):
    groups, chips = n // 2, t // 2
    i, k = lax.axis_index("layer"), lax.axis_index("tok")
    g, p = i // 2, i % 2
    y, c = k // 2, k % 2
    other_layer = 2 * g + 1 - p
    other_core = 2 * y + 1 - c
    rows, depth = acts.shape[1], wenc_v.shape[0]
    features, width = wdec_v.shape[1], wdec_v.shape[2]
    half_f, half_w = features // 2, width // 2
    tokens = rows * t
    first = 2 * g
    count = n - first
    whole = n - max(0, min(n // 2, n - 4))

    def remote(src, dst, send, recv, layer, tok):
        return pltpu.make_async_remote_copy(
            src_ref=src, dst_ref=dst, send_sem=send, recv_sem=recv,
            device_id=(layer, tok), device_id_type=MESH,
        )

    wenc_copy = pltpu.make_async_copy(w_enc.at[0], wenc_v, s_wenc)
    wenc_copy.start()
    own_cols = pl.ds(pl.multiple_of(k * depth, depth), depth)
    own_rows = pl.ds(pl.multiple_of(k * rows, rows), rows)
    acts_copy = pltpu.make_async_copy(acts.at[0, :, own_cols], acts_v.at[own_rows, :], s_acts)
    acts_copy.start()

    def dec_copy(j):
        return pltpu.make_async_copy(w_dec.at[0, j], wdec_v.at[j], s_wdec.at[j])

    barrier = pltpu.get_barrier_semaphore()
    for step in range(1, t):
        pl.semaphore_signal(
            barrier, inc=1, device_id=(i, lax.rem(k + step, t)), device_id_type=MESH
        )
    pl.semaphore_signal(barrier, inc=1, device_id=(other_layer, k), device_id_type=MESH)

    @pl.when(g > 0)
    def _():
        pl.semaphore_signal(barrier, inc=1, device_id=(i - 2, k), device_id_type=MESH)

    @pl.when(g < groups - 1)
    def _():
        pl.semaphore_signal(barrier, inc=1, device_id=(i + 2, k), device_id_type=MESH)

    @pl.when(g == 0)
    def _():
        fwd_in[...] = jnp.zeros_like(fwd_in)

    for q in range(2):
        bwd_in[first + q] = jnp.zeros(bwd_in.shape[1:], BF)

    linked = (g > 0).astype(jnp.int32) + (g < groups - 1).astype(jnp.int32)
    pl.semaphore_wait(barrier, t + linked)

    def acts_send(peer):
        cols = pl.ds(pl.multiple_of(peer * depth, depth), depth)
        return remote(
            acts.at[0, :, cols], acts_v.at[own_rows, :], a_send.at[peer], a_recv.at[k], i, peer
        )

    def acts_land(peer):
        lines = pl.ds(pl.multiple_of(peer * rows, rows), rows)
        return remote(
            acts.at[0, :, own_cols], acts_v.at[lines, :], a_send.at[peer], a_recv.at[peer], i, peer
        )

    for step in range(1, t):
        acts_send(lax.rem(k + step, t)).start()

    def start_dec(q, _):
        dec_copy(n - 1 - q).start()
        return 0

    lax.fori_loop(0, count, start_dec, 0)
    wenc_copy.wait()
    acts_copy.wait()
    for step in range(1, t):
        acts_land(lax.rem(k + step, t)).wait_recv()

    for h in range(2):
        pre[h] = jnp.dot(
            acts_v[...], wenc_v[:, h * half_f:(h + 1) * half_f], preferred_element_type=F32
        )
    pre_copy = remote(pre.at[1 - c], pre_in, p_sem.at[0], p_sem.at[1], i, other_core)
    pre_copy.start()
    pre_copy.wait_recv()
    chip_sum = pre[c] + pre_in[...]
    pair_out[...] = chip_sum.astype(BF)

    own_half = pl.ds(pl.multiple_of(c * half_f, half_f), half_f)

    def pair_send(peer):
        return remote(pair_out, pair_in.at[y], y_send.at[peer], y_recv.at[y], i, 2 * peer + c)

    def pair_land(peer):
        return remote(pair_out, pair_in.at[peer], y_send.at[peer], y_recv.at[peer], i, 2 * peer + c)

    for step in range(1, chips):
        pair_send(lax.rem(y + step, chips)).start()
    pre_in[...] = chip_sum + bias[:, own_half]
    for step in range(1, chips):
        peer = lax.rem(y + step, chips)
        pair_land(peer).wait_recv()
        pre_in[...] += pair_in[peer].astype(F32)
    codes_v[c] = jnp.maximum(pre_in[...], 0.0).astype(BF)
    codes_copy = remote(codes_v.at[c], codes_v.at[c], c_sem.at[0], c_sem.at[1], i, other_core)
    codes_copy.start()
    codes_land = remote(
        codes_v.at[c], codes_v.at[1 - c], c_sem.at[0], c_sem.at[1], i, other_core
    )
    codes_land.wait_recv()

    def mix(j):
        return remote(mix_out.at[j], mix_in.at[j], m_send.at[j], m_recv.at[j], other_layer, k)

    def ahead(j):
        return remote(fwd_out.at[j], fwd_in.at[j], f_send.at[j], f_recv.at[j], i + 2, k)

    def back(j):
        return remote(bwd_out.at[j], bwd_in.at[j], b_send.at[j], b_recv.at[j], i - 2, k)

    def share(j):
        return remote(err_v.at[j, p], err_v.at[j, p], e_send.at[j], e_recv.at[j], other_layer, k)

    def share_land(j):
        return remote(
            err_v.at[j, p], err_v.at[j, 1 - p], e_send.at[j], e_recv.at[j], other_layer, k
        )

    def direct(j):
        return remote(err_v.at[j], err_v.at[j], d_send.at[j], d_recv.at[j], i - 2, k)

    def mix_leaves(j):
        return (j > first) | ((p == 0) & (g > 0))

    def mix_lands(j):
        return (j > first) | ((p == 1) & (g > 0))

    def share_leaves(j):
        return ((j > first) | ((p == 1) & (g > 0))) & ((g > 0) | (j < whole))

    def share_lands(j):
        return ((j > first) | ((p == 0) & (g > 0))) & ((g > 0) | (j < whole))

    def decode(q, _):
        j = n - 1 - q
        dec_copy(j).wait()
        both = []
        for h in range(2):
            cols = slice(h * half_w, (h + 1) * half_w)
            product = jnp.dot(
                codes_v[0], wdec_v[j, :half_f, cols], preferred_element_type=F32
            ) + jnp.dot(codes_v[1], wdec_v[j, half_f:, cols], preferred_element_type=F32)
            product = jnp.where(j >= i, product, 0.0)
            goal = targets[0, :, cols].astype(F32)
            both.append(product - jnp.where(j == i, goal, 0.0))
        held[j] = jnp.where(p == 0, both[0], both[1])
        mix_out[j] = jnp.where(p == 0, both[1], both[0]).astype(BF)

        @pl.when(mix_leaves(j))
        def _():
            mix(j).start()

        @pl.when((g == 0) & (j == first) & (p == 0))
        def _():
            err_v[j, 1] = mix_out[j]

        return 0

    lax.fori_loop(0, count, decode, 0)
    for h in range(2):
        codes[h] = codes_v[h].T
    cg[...] = jnp.zeros_like(cg)

    def gather_pair(j):
        @pl.when(mix_lands(j))
        def _():
            mix(j).wait_recv()
            held[j] = held[j] + mix_in[j].astype(F32)

    def wait_ahead(j):
        @pl.when(g > 0)
        def _():
            ahead(j).wait_recv()

    def wait_back(j):
        @pl.when(j >= first + 2)
        def _():
            back(j).wait_recv()

    def send_ahead(j):
        @pl.when(j >= first + 2)
        def _():
            fwd_out[j] = (held[j] + fwd_in[j].astype(F32)).astype(BF)
            ahead(j).start()

    def send_back(j):
        @pl.when((g > 1) | ((g == 1) & (j < whole)))
        def _():
            bwd_out[j] = (held[j] + bwd_in[j].astype(F32)).astype(BF)
            back(j).start()

    def finish(j):
        total = held[j] + fwd_in[j].astype(F32) + bwd_in[j].astype(F32)
        err_v[j, p] = total.astype(BF)

        @pl.when(share_leaves(j))
        def _():
            share(j).start()

    def arrive(j):
        @pl.when(share_lands(j))
        def _():
            share_land(j).wait_recv()

        @pl.when((g == 0) & (j >= whole))
        def _():
            direct(j).wait_recv()

        @pl.when((g == 1) & (j >= whole))
        def _():
            direct(j).start()

    early = (g > 0) & (g < groups // 2)

    @pl.when(g == 0)
    def _():
        def one(q, _):
            j = n - 1 - q
            gather_pair(j)
            send_ahead(j)
            return 0

        def two(q, _):
            j = whole - 1 - q
            wait_back(j)
            finish(j)
            return 0

        lax.fori_loop(0, n, one, 0)
        lax.fori_loop(0, whole, two, 0)

    @pl.when(early)
    def _():
        def one(q, _):
            @pl.when(q < count)
            def _():
                j = n - 1 - q
                gather_pair(j)
                wait_ahead(j)
                send_ahead(j)
                wait_back(j)
                send_back(j)
                finish(j)

            @pl.when(q >= 2)
            def _():
                arrive(n + 1 - q)

            return 0

        lax.fori_loop(0, count + 2, one, 0)

    @pl.when((g > 0) & (g >= groups // 2))
    def _():
        def one(q, _):
            j = n - 1 - q
            gather_pair(j)
            wait_back(j)
            send_back(j)
            return 0

        def two(q, _):
            j = n - 1 - q
            wait_ahead(j)
            send_ahead(j)
            finish(j)
            return 0

        lax.fori_loop(0, count, one, 0)
        lax.fori_loop(0, count, two, 0)

    def backward(q, _):
        j = n - 1 - q
        keep = j >= i

        @pl.when(jnp.logical_not(early))
        def _():
            arrive(j)

        @pl.when(jnp.logical_not(keep))
        def _():
            errs[j] = jnp.zeros(errs.shape[1:], BF)

        @pl.when(keep)
        def _():
            errs[j] = err_v[j]
            nt = (((1,), (1,)), ((), ()))
            part = lax.dot_general(
                err_v[j, 0], wdec_v[j, :, :half_w], nt, preferred_element_type=F32
            ) + lax.dot_general(
                err_v[j, 1], wdec_v[j, :, half_w:], nt, preferred_element_type=F32
            )
            cg[...] += part.reshape(cg.shape)

        return 0

    lax.fori_loop(0, count, backward, 0)

    def blank(j, _):
        errs[j] = jnp.zeros(errs.shape[1:], BF)
        return 0

    lax.fori_loop(0, first, blank, 0)

    cg_copy = remote(cg.at[:, 1 - c], cg_in, g_sem.at[0], g_sem.at[1], i, other_core)
    cg_copy.start()
    cg_copy.wait_recv()

    def far_send(peer):
        return remote(
            cg_out.at[peer], cg_far.at[y], gy_send.at[peer], gy_recv.at[y], i, 2 * peer + c
        )

    def far_land(peer):
        return remote(
            cg_out.at[peer], cg_far.at[peer], gy_send.at[peer], gy_recv.at[peer], i, 2 * peer + c
        )

    for step in range(1, chips):
        peer = lax.rem(y + step, chips)
        cg_out[peer] = (cg[peer, c] + cg_in[peer]).astype(BF)
        far_send(peer).start()
    grads[...] = cg[y, c] + cg_in[y]
    for step in range(1, chips):
        peer = lax.rem(y + step, chips)
        far_land(peer).wait_recv()
        grads[...] += cg_far[peer].astype(F32)

    for step in range(1, t):
        acts_send(lax.rem(k + step, t)).wait_send()
    pre_copy.wait_send()
    codes_copy.wait_send()
    cg_copy.wait_send()
    for step in range(1, chips):
        peer = lax.rem(y + step, chips)
        pair_send(peer).wait_send()
        far_send(peer).wait_send()

    def drain(q, _):
        j = n - 1 - q

        @pl.when(mix_leaves(j))
        def _():
            mix(j).wait_send()

        @pl.when(share_leaves(j))
        def _():
            share(j).wait_send()

        @pl.when((g == 1) & (j >= whole))
        def _():
            direct(j).wait_send()

        @pl.when(j >= first + 2)
        def _():
            ahead(j).wait_send()

        @pl.when((g > 1) | ((g == 1) & (j < whole)))
        def _():
            back(j).wait_send()

        return 0

    lax.fori_loop(0, count, drain, 0)


def weight_grads(codes, errs, grads_in, dec, grads):
    grads[...] = grads_in[...]
    half_f, half_w = codes.shape[1], errs.shape[3]
    for a in range(2):
        for b in range(2):
            dec[0, 0, a * half_f:(a + 1) * half_f, b * half_w:(b + 1) * half_w] = jnp.dot(
                codes[a], errs[0, b], preferred_element_type=F32
            ).astype(BF)


def local(acts, w_enc, b_enc, w_dec, targets):
    n, t = lax.axis_size("layer"), lax.axis_size("tok")
    _, rows, model = acts.shape
    _, depth, features = w_enc.shape
    width = w_dec.shape[3]
    tokens = rows * t
    half_f, half_w = features // 2, width // 2
    chips = t // 2
    vmem = pl.BlockSpec(memory_space=pltpu.VMEM)
    hbm = pl.BlockSpec(memory_space=pl.ANY)
    block = (n, tokens, half_w)
    dma = pltpu.SemaphoreType.DMA
    codes, errs, grads = pl.pallas_call(
        functools.partial(exchange, n, t),
        out_shape=(
            jax.ShapeDtypeStruct((2, half_f, tokens), BF),
            jax.ShapeDtypeStruct((n, 2, tokens, half_w), BF),
            jax.ShapeDtypeStruct((rows, features), F32),
        ),
        in_specs=[hbm, hbm, vmem, hbm, vmem],
        out_specs=(vmem, vmem, vmem),
        scratch_shapes=[
            pltpu.VMEM((tokens, depth), BF),
            pltpu.VMEM((depth, features), BF),
            pltpu.VMEM((n, features, width), BF),
            pltpu.VMEM((2, tokens, half_f), F32),
            pltpu.VMEM((tokens, half_f), F32),
            pltpu.VMEM((tokens, half_f), BF),
            pltpu.VMEM((chips, tokens, half_f), BF),
            pltpu.VMEM((2, tokens, half_f), BF),
            pltpu.VMEM(block, F32),
            pltpu.VMEM(block, BF),
            pltpu.VMEM(block, BF),
            pltpu.VMEM(block, BF),
            pltpu.VMEM(block, BF),
            pltpu.VMEM(block, BF),
            pltpu.VMEM(block, BF),
            pltpu.VMEM((n, 2, tokens, half_w), BF),
            pltpu.VMEM((chips, 2, rows, features), F32),
            pltpu.VMEM((chips, rows, features), F32),
            pltpu.VMEM((chips, rows, features), BF),
            pltpu.VMEM((chips, rows, features), BF),
            dma, dma((n,)), dma, dma((t,)), dma((t,)), dma((2,)),
            dma((chips,)), dma((chips,)), dma((2,)),
            dma((n,)), dma((n,)), dma((n,)), dma((n,)), dma((n,)), dma((n,)),
            dma((n,)), dma((n,)), dma((n,)), dma((n,)), dma((2,)), dma((chips,)), dma((chips,)),
        ],
        compiler_params=pltpu.CompilerParams(
            collective_id=0, has_side_effects=True, vmem_limit_bytes=56 * 2**20
        ),
        name="exchange",
    )(acts, w_enc, b_enc, w_dec, targets)
    dec, code_share = pl.pallas_call(
        weight_grads,
        grid=(n,),
        out_shape=(
            jax.ShapeDtypeStruct((1, n, features, width), BF),
            jax.ShapeDtypeStruct((rows, features), F32),
        ),
        in_specs=[
            pl.BlockSpec((2, half_f, tokens), lambda j: (0, 0, 0)),
            pl.BlockSpec((1, 2, tokens, half_w), lambda j: (j, 0, 0, 0)),
            pl.BlockSpec((rows, features), lambda j: (0, 0)),
        ],
        out_specs=(
            pl.BlockSpec((1, 1, features, width), lambda j: (0, j, 0, 0)),
            pl.BlockSpec((rows, features), lambda j: (0, 0)),
        ),
        compiler_params=pltpu.CompilerParams(vmem_limit_bytes=58 * 2**20),
        name="weight_grads",
    )(codes, errs, grads)
    return (code_share[None], dec)


def solution(mesh):
    return jax.shard_map(
        local,
        mesh=mesh,
        in_specs=(
            P("layer", "tok", None),
            P("layer", "tok", None),
            P("layer", None),
            P("layer", None, None, "tok"),
            P("layer", None, "tok"),
        ),
        out_specs=(P("layer", "tok", None), P("layer", None, None, "tok")),
        check_vma=False,
    )
```

```python
import functools

import jax
import jax.numpy as jnp
from jax import lax
from jax.experimental import pallas as pl
from jax.experimental.pallas import tpu as pltpu
from jax.sharding import PartitionSpec as P

MESH = pl.DeviceIdType.MESH
BF = jnp.bfloat16
F32 = jnp.float32


def exchange(
    n, t, acts, w_enc, bias, w_dec, targets,
    codes, errs, grads,
    acts_v, wenc_v, wdec_v, pre, pre_in, pair_out, pair_in, codes_v,
    held, mix_out, mix_in, fwd_out, fwd_in, bwd_out, bwd_in, err_v,
    cg, cg_in, cg_out, cg_far,
    s_wenc, s_wdec, s_acts, a_send, a_recv, p_sem, y_send, y_recv, c_sem,
    m_send, m_recv, f_send, f_recv, b_send, b_recv, e_send, e_recv, d_send, d_recv, g_sem, gy_send, gy_recv,
):
    groups, chips = n // 2, t // 2
    i, k = lax.axis_index("layer"), lax.axis_index("tok")
    g, p = i // 2, i % 2
    y, c = k // 2, k % 2
    other_layer = 2 * g + 1 - p
    other_core = 2 * y + 1 - c
    rows, depth = acts.shape[1], wenc_v.shape[0]
    features, width = wdec_v.shape[1], wdec_v.shape[2]
    half_f, half_w = features // 2, width // 2
    tokens = rows * t
    first = 2 * g
    count = n - first
    whole = n - max(0, min(n // 4, n - 4))

    def remote(src, dst, send, recv, layer, tok):
        return pltpu.make_async_remote_copy(
            src_ref=src, dst_ref=dst, send_sem=send, recv_sem=recv,
            device_id=(layer, tok), device_id_type=MESH,
        )

    wenc_copy = pltpu.make_async_copy(w_enc.at[0], wenc_v, s_wenc)
    wenc_copy.start()
    own_cols = pl.ds(pl.multiple_of(k * depth, depth), depth)
    own_rows = pl.ds(pl.multiple_of(k * rows, rows), rows)
    acts_copy = pltpu.make_async_copy(acts.at[0, :, own_cols], acts_v.at[own_rows, :], s_acts)
    acts_copy.start()

    def dec_copy(j):
        return pltpu.make_async_copy(w_dec.at[0, j], wdec_v.at[j], s_wdec.at[j])

    barrier = pltpu.get_barrier_semaphore()
    for step in range(1, t):
        pl.semaphore_signal(
            barrier, inc=1, device_id=(i, lax.rem(k + step, t)), device_id_type=MESH
        )
    pl.semaphore_signal(barrier, inc=1, device_id=(other_layer, k), device_id_type=MESH)

    @pl.when(g > 0)
    def _():
        pl.semaphore_signal(barrier, inc=1, device_id=(i - 2, k), device_id_type=MESH)

    @pl.when(g < groups - 1)
    def _():
        pl.semaphore_signal(barrier, inc=1, device_id=(i + 2, k), device_id_type=MESH)

    @pl.when(g == 0)
    def _():
        fwd_in[...] = jnp.zeros_like(fwd_in)

    for q in range(2):
        bwd_in[first + q] = jnp.zeros(bwd_in.shape[1:], BF)

    linked = (g > 0).astype(jnp.int32) + (g < groups - 1).astype(jnp.int32)
    pl.semaphore_wait(barrier, t + linked)

    def acts_send(peer):
        cols = pl.ds(pl.multiple_of(peer * depth, depth), depth)
        return remote(
            acts.at[0, :, cols], acts_v.at[own_rows, :], a_send.at[peer], a_recv.at[k], i, peer
        )

    def acts_land(peer):
        lines = pl.ds(pl.multiple_of(peer * rows, rows), rows)
        return remote(
            acts.at[0, :, own_cols], acts_v.at[lines, :], a_send.at[peer], a_recv.at[peer], i, peer
        )

    for step in range(1, t):
        acts_send(lax.rem(k + step, t)).start()

    def start_dec(q, _):
        dec_copy(n - 1 - q).start()
        return 0

    lax.fori_loop(0, count, start_dec, 0)
    wenc_copy.wait()
    acts_copy.wait()
    for step in range(1, t):
        acts_land(lax.rem(k + step, t)).wait_recv()

    for h in range(2):
        pre[h] = jnp.dot(
            acts_v[...], wenc_v[:, h * half_f:(h + 1) * half_f], preferred_element_type=F32
        )
    pre_copy = remote(pre.at[1 - c], pre_in, p_sem.at[0], p_sem.at[1], i, other_core)
    pre_copy.start()
    pre_copy.wait_recv()
    chip_sum = pre[c] + pre_in[...]
    pair_out[...] = chip_sum.astype(BF)

    own_half = pl.ds(pl.multiple_of(c * half_f, half_f), half_f)

    def pair_send(peer):
        return remote(pair_out, pair_in.at[y], y_send.at[peer], y_recv.at[y], i, 2 * peer + c)

    def pair_land(peer):
        return remote(pair_out, pair_in.at[peer], y_send.at[peer], y_recv.at[peer], i, 2 * peer + c)

    for step in range(1, chips):
        pair_send(lax.rem(y + step, chips)).start()
    pre_in[...] = chip_sum + bias[:, own_half]
    for step in range(1, chips):
        peer = lax.rem(y + step, chips)
        pair_land(peer).wait_recv()
        pre_in[...] += pair_in[peer].astype(F32)
    codes_v[c] = jnp.maximum(pre_in[...], 0.0).astype(BF)
    codes_copy = remote(codes_v.at[c], codes_v.at[c], c_sem.at[0], c_sem.at[1], i, other_core)
    codes_copy.start()
    codes_land = remote(
        codes_v.at[c], codes_v.at[1 - c], c_sem.at[0], c_sem.at[1], i, other_core
    )
    codes_land.wait_recv()

    def mix(j):
        return remote(mix_out.at[j], mix_in.at[j], m_send.at[j], m_recv.at[j], other_layer, k)

    def ahead(j):
        return remote(fwd_out.at[j], fwd_in.at[j], f_send.at[j], f_recv.at[j], i + 2, k)

    def back(j):
        return remote(bwd_out.at[j], bwd_in.at[j], b_send.at[j], b_recv.at[j], i - 2, k)

    def share(j):
        return remote(err_v.at[j, p], err_v.at[j, p], e_send.at[j], e_recv.at[j], other_layer, k)

    def share_land(j):
        return remote(
            err_v.at[j, p], err_v.at[j, 1 - p], e_send.at[j], e_recv.at[j], other_layer, k
        )

    def direct(j):
        return remote(err_v.at[j], err_v.at[j], d_send.at[j], d_recv.at[j], i - 2, k)

    def mix_leaves(j):
        return (j > first) | ((p == 0) & (g > 0))

    def mix_lands(j):
        return (j > first) | ((p == 1) & (g > 0))

    def share_leaves(j):
        return ((j > first) | ((p == 1) & (g > 0))) & ((g > 0) | (j < whole))

    def share_lands(j):
        return ((j > first) | ((p == 0) & (g > 0))) & ((g > 0) | (j < whole))

    def decode(j):
        dec_copy(j).wait()
        both = []
        for h in range(2):
            cols = slice(h * half_w, (h + 1) * half_w)
            product = jnp.dot(
                codes_v[0], wdec_v[j, :half_f, cols], preferred_element_type=F32
            ) + jnp.dot(codes_v[1], wdec_v[j, half_f:, cols], preferred_element_type=F32)
            product = jnp.where(j >= i, product, 0.0)
            goal = targets[0, :, cols].astype(F32)
            both.append(product - jnp.where(j == i, goal, 0.0))
        held[j] = jnp.where(p == 0, both[0], both[1])
        mix_out[j] = jnp.where(p == 0, both[1], both[0]).astype(BF)

        @pl.when(j + 4 < n)
        def _():
            mix(j + 4).wait_send()

        @pl.when(mix_leaves(j))
        def _():
            mix(j).start()

        @pl.when((g == 0) & (j == first) & (p == 0))
        def _():
            err_v[j, 1] = mix_out[j]


    def gather_pair(j):
        @pl.when(mix_lands(j))
        def _():
            mix(j).wait_recv()
            held[j] = held[j] + mix_in[j].astype(F32)

    def wait_ahead(j):
        @pl.when(g > 0)
        def _():
            ahead(j).wait_recv()

    def wait_back(j):
        @pl.when(j >= first + 2)
        def _():
            back(j).wait_recv()

    def send_ahead(j):
        @pl.when(j >= first + 2)
        def _():
            fwd_out[j] = (held[j] + fwd_in[j].astype(F32)).astype(BF)
            ahead(j).start()

    def send_back(j):
        @pl.when((g > 1) | ((g == 1) & (j < whole)))
        def _():
            bwd_out[j] = (held[j] + bwd_in[j].astype(F32)).astype(BF)
            back(j).start()

    def finish(j):
        total = held[j] + fwd_in[j].astype(F32) + bwd_in[j].astype(F32)
        err_v[j, p] = total.astype(BF)

        @pl.when(share_leaves(j))
        def _():
            share(j).start()

    def arrive(j):
        @pl.when(share_lands(j))
        def _():
            share_land(j).wait_recv()

        @pl.when((g == 0) & (j >= whole))
        def _():
            direct(j).wait_recv()

        @pl.when((g == 1) & (j >= whole))
        def _():
            direct(j).start()

    early = (g > 0) & (g < groups // 2)

    lower = g < groups // 2
    lag_one, lag_two, lag_three = 4, 7, 9

    def step(q, _):
        @pl.when(q < count)
        def _():
            decode(n - 1 - q)

        @pl.when((q >= lag_one) & (q < count + lag_one))
        def _():
            j = n - 1 - q + lag_one
            gather_pair(j)

            @pl.when(lower)
            def _():
                wait_ahead(j)
                send_ahead(j)

            @pl.when(jnp.logical_not(lower))
            def _():
                wait_back(j)
                send_back(j)

        @pl.when((q >= lag_two) & (q < count + lag_two))
        def _():
            j = n - 1 - q + lag_two

            @pl.when(lower & ((g > 0) | (j < whole)))
            def _():
                wait_back(j)
                send_back(j)
                finish(j)

            @pl.when(jnp.logical_not(lower))
            def _():
                wait_ahead(j)
                send_ahead(j)
                finish(j)

        @pl.when(early & (q >= lag_three))
        def _():
            arrive(n - 1 - q + lag_three)

        return 0

    lax.fori_loop(0, count + lag_three, step, 0)
    for h in range(2):
        codes[h] = codes_v[h].T
    cg[...] = jnp.zeros_like(cg)

    def backward(q, _):
        j = n - 1 - q
        keep = j >= i

        @pl.when(jnp.logical_not(early))
        def _():
            arrive(j)

        @pl.when(jnp.logical_not(keep))
        def _():
            errs[j] = jnp.zeros(errs.shape[1:], BF)

        @pl.when(keep)
        def _():
            errs[j] = err_v[j]
            nt = (((1,), (1,)), ((), ()))
            part = lax.dot_general(
                err_v[j, 0], wdec_v[j, :, :half_w], nt, preferred_element_type=F32
            ) + lax.dot_general(
                err_v[j, 1], wdec_v[j, :, half_w:], nt, preferred_element_type=F32
            )
            cg[...] += part.reshape(cg.shape)

        return 0

    lax.fori_loop(0, count, backward, 0)

    def blank(j, _):
        errs[j] = jnp.zeros(errs.shape[1:], BF)
        return 0

    lax.fori_loop(0, first, blank, 0)

    cg_copy = remote(cg.at[:, 1 - c], cg_in, g_sem.at[0], g_sem.at[1], i, other_core)
    cg_copy.start()
    cg_copy.wait_recv()

    def far_send(peer):
        return remote(
            cg_out.at[peer], cg_far.at[y], gy_send.at[peer], gy_recv.at[y], i, 2 * peer + c
        )

    def far_land(peer):
        return remote(
            cg_out.at[peer], cg_far.at[peer], gy_send.at[peer], gy_recv.at[peer], i, 2 * peer + c
        )

    for step in range(1, chips):
        peer = lax.rem(y + step, chips)
        cg_out[peer] = (cg[peer, c] + cg_in[peer]).astype(BF)
        far_send(peer).start()
    grads[...] = cg[y, c] + cg_in[y]
    for step in range(1, chips):
        peer = lax.rem(y + step, chips)
        far_land(peer).wait_recv()
        grads[...] += cg_far[peer].astype(F32)

    for step in range(1, t):
        acts_send(lax.rem(k + step, t)).wait_send()
    pre_copy.wait_send()
    codes_copy.wait_send()
    cg_copy.wait_send()
    for step in range(1, chips):
        peer = lax.rem(y + step, chips)
        pair_send(peer).wait_send()
        far_send(peer).wait_send()

    def drain(q, _):
        j = n - 1 - q

        @pl.when(mix_leaves(j) & (j < first + 4))
        def _():
            mix(j).wait_send()

        @pl.when(share_leaves(j))
        def _():
            share(j).wait_send()

        @pl.when((g == 1) & (j >= whole))
        def _():
            direct(j).wait_send()

        @pl.when(j >= first + 2)
        def _():
            ahead(j).wait_send()

        @pl.when((g > 1) | ((g == 1) & (j < whole)))
        def _():
            back(j).wait_send()

        return 0

    lax.fori_loop(0, count, drain, 0)


def weight_grads(codes, errs, grads_in, dec, grads):
    grads[...] = grads_in[...]
    half_f, half_w = codes.shape[1], errs.shape[3]
    for j in range(errs.shape[0]):
        both = jnp.concatenate([errs[j, 0], errs[j, 1]], axis=1)
        for a in range(2):
            dec[0, j, a * half_f:(a + 1) * half_f, :] = jnp.dot(
                codes[a], both, preferred_element_type=F32
            ).astype(BF)


def local(acts, w_enc, b_enc, w_dec, targets):
    n, t = lax.axis_size("layer"), lax.axis_size("tok")
    _, rows, model = acts.shape
    _, depth, features = w_enc.shape
    width = w_dec.shape[3]
    tokens = rows * t
    half_f, half_w = features // 2, width // 2
    chips = t // 2
    vmem = pl.BlockSpec(memory_space=pltpu.VMEM)
    hbm = pl.BlockSpec(memory_space=pl.ANY)
    block = (n, tokens, half_w)
    dma = pltpu.SemaphoreType.DMA
    codes, errs, grads = pl.pallas_call(
        functools.partial(exchange, n, t),
        out_shape=(
            jax.ShapeDtypeStruct((2, half_f, tokens), BF),
            jax.ShapeDtypeStruct((n, 2, tokens, half_w), BF),
            jax.ShapeDtypeStruct((rows, features), F32),
        ),
        in_specs=[hbm, hbm, vmem, hbm, vmem],
        out_specs=(vmem, vmem, vmem),
        scratch_shapes=[
            pltpu.VMEM((tokens, depth), BF),
            pltpu.VMEM((depth, features), BF),
            pltpu.VMEM((n, features, width), BF),
            pltpu.VMEM((2, tokens, half_f), F32),
            pltpu.VMEM((tokens, half_f), F32),
            pltpu.VMEM((tokens, half_f), BF),
            pltpu.VMEM((chips, tokens, half_f), BF),
            pltpu.VMEM((2, tokens, half_f), BF),
            pltpu.VMEM(block, F32),
            pltpu.VMEM(block, BF),
            pltpu.VMEM(block, BF),
            pltpu.VMEM(block, BF),
            pltpu.VMEM(block, BF),
            pltpu.VMEM(block, BF),
            pltpu.VMEM(block, BF),
            pltpu.VMEM((n, 2, tokens, half_w), BF),
            pltpu.VMEM((chips, 2, rows, features), F32),
            pltpu.VMEM((chips, rows, features), F32),
            pltpu.VMEM((chips, rows, features), BF),
            pltpu.VMEM((chips, rows, features), BF),
            dma, dma((n,)), dma, dma((t,)), dma((t,)), dma((2,)),
            dma((chips,)), dma((chips,)), dma((2,)),
            dma((n,)), dma((n,)), dma((n,)), dma((n,)), dma((n,)), dma((n,)),
            dma((n,)), dma((n,)), dma((n,)), dma((n,)), dma((2,)), dma((chips,)), dma((chips,)),
        ],
        compiler_params=pltpu.CompilerParams(
            collective_id=0, has_side_effects=True, vmem_limit_bytes=56 * 2**20
        ),
        name="exchange",
    )(acts, w_enc, b_enc, w_dec, targets)
    dec, code_share = pl.pallas_call(
        weight_grads,
        grid=(n // 2,),
        out_shape=(
            jax.ShapeDtypeStruct((1, n, features, width), BF),
            jax.ShapeDtypeStruct((rows, features), F32),
        ),
        in_specs=[
            pl.BlockSpec((2, half_f, tokens), lambda j: (0, 0, 0)),
            pl.BlockSpec((2, 2, tokens, half_w), lambda j: (j, 0, 0, 0)),
            pl.BlockSpec((rows, features), lambda j: (0, 0)),
        ],
        out_specs=(
            pl.BlockSpec((1, 2, features, width), lambda j: (0, j, 0, 0)),
            pl.BlockSpec((rows, features), lambda j: (0, 0)),
        ),
        compiler_params=pltpu.CompilerParams(vmem_limit_bytes=58 * 2**20),
        name="weight_grads",
    )(codes, errs, grads)
    return (code_share[None], dec)


def solution(mesh):
    return jax.shard_map(
        local,
        mesh=mesh,
        in_specs=(
            P("layer", "tok", None),
            P("layer", "tok", None),
            P("layer", None),
            P("layer", None, None, "tok"),
            P("layer", None, "tok"),
        ),
        out_specs=(P("layer", "tok", None), P("layer", None, None, "tok")),
        check_vma=False,
    )
```
